32 devices in a mesh: ctx: 8 (over z, core), tp: 2 (over x), run: 2 (over y).
Axes of the slice: x: 2, y: 2, z: 4, core: 2. Of those that a mesh axis runs over, the one named last changes fastest.
Arguments:
- tokens: bfloat16 [4096, 5120], P(('run', 'ctx')), parts along dimension 0, may hold values from -28 to 28
- block_order: int32 [32], replicated, may hold values from 0 to 31, each once
- doc_lengths: int32 [16], replicated, may hold values from 1 to 512, 2048 in all
- patch_pos: int32 [512], P(('run', 'ctx')), parts along dimension 0, may hold values from 0 to 2047, as said below
- clean_rows: bfloat16 [512, 5120], P(('run', 'ctx')), parts along dimension 0, may hold values from -6 to 6
- w_query: bfloat16 [5120, 5120], P(None, 'tp'), may hold values from -0.078125 to 0.078125
- q_bias: bfloat16 [5120], P('tp'), may hold values from -3 to 3
- w_key: bfloat16 [5120, 1024], P(None, 'tp'), may hold values from -0.078125 to 0.078125
- k_bias: bfloat16 [1024], P('tp'), may hold values from -3 to 3
- w_value: bfloat16 [5120, 1024], P(None, 'tp'), may hold values from -0.078125 to 0.078125
- v_bias: bfloat16 [1024], P('tp'), may hold values from -3 to 3
Outputs:
- attended: bfloat16 [4096, 5120], P(('run', 'ctx'), 'tp'), parts along dimension 0
The draws below stay inside these ranges and needn't reach their ends.
There are 2 independent parts, one for each index of `run`. The reference program is written for one: setup_inputs(seed, part) draws one part's arguments, and reference() takes and returns one part's arrays. A program takes and returns all parts, laid end to end along the dimension named above; an argument that names none is the same for every part. Nothing has to cross between parts.
Inputs may be any that keep to these rules, and one draw needn't show every extreme that they name: `block_order`: every block index appears exactly once. `doc_lengths`: the lengths sum to 2048 and the largest equals 512. `patch_pos`: the 256 positions are distinct positions of the sequence, the first and the last position among them.
All inputs are finite; a program needn't handle non-finite values.
Results may differ from the reference program's by a relative error of at most 0.0076.
Values may be sent and summed in bfloat16 or wider, within the bound.
A program may use at most 128 MiB of HBM per device.

```python
import math
import jax
import jax.numpy as jnp
import numpy as np
from jax import lax

D = 5120
QH = 40
KVH = 8
HD = 128
BLOCK = 64
NDOC = 16
TOKENS = 2048
NBLOCKS = 32
PATCHES = 256
MOST_DOC = 512


def draw_tokens(key, part):
    return jnp.clip(jax.random.normal(key, (TOKENS, D), jnp.float32), -6.0, 6.0).astype(jnp.bfloat16)


def draw_patch_pos(key, part):
    inner = jax.random.permutation(jax.random.fold_in(key, 7), TOKENS - 2)[:PATCHES - 2].astype(jnp.int32) + 1
    ends = jnp.array([0, TOKENS - 1], dtype=jnp.int32)
    joined = jnp.concatenate([ends, inner])
    return jax.random.permutation(jax.random.fold_in(key, 11), joined).astype(jnp.int32)


def block_scale(own_key, dims, cuts, smallest, high):
    level = 1.0
    for axis_at, blocks in cuts:
        draws = jax.random.uniform(jax.random.fold_in(jax.random.fold_in(own_key, 6), axis_at), (blocks,), jnp.float32, smallest / len(cuts), high / len(cuts))
        level = level * jnp.repeat(jnp.exp(draws), dims[axis_at] // blocks).reshape((-1,) + (1,) * (len(dims) - 1 - axis_at))
    return level


def profile(number_of, total, bound, skew):
    loads = [(1 << 20) // math.isqrt(standing ** skew) + 1 for standing in range(2, number_of + 1)]
    spare, given = total - bound - (number_of - 1), [1] * (number_of - 1)
    while spare > 0:
        movable = [i for i in range(number_of - 1) if given[i] < bound]
        mass, left = sum([loads[i] for i in movable]), spare
        for i in movable:
            addition = min(bound - given[i], max(1, left * loads[i] // mass), spare)
            given[i] = given[i] + addition
            spare = spare - addition
    return np.array([bound] + given)


def uneven(own_key, amount, total, bound, skew):
    if amount == 2:
        one = jax.random.randint(own_key, (), max(1, total - bound), min(bound, total - 1) + 1)
        return jnp.stack([one, total - one])
    tallies = jnp.asarray(profile(amount, total, bound, skew), jnp.int32)
    twos = (amount - 1) // 2
    giver, taker = tallies[1:1 + 2 * twos:2], tallies[2:2 + 2 * twos:2]
    slack = jnp.minimum(giver - 1, bound - taker)
    moved = jax.random.randint(jax.random.fold_in(own_key, 1), (twos,), 0, 1 << 20) % (slack + 1)
    tallies = tallies.at[1:1 + 2 * twos:2].set(giver - moved).at[2:2 + 2 * twos:2].set(taker + moved)
    return tallies[jax.random.permutation(jax.random.fold_in(own_key, 2), amount)]


def scatter_about(rng, shape, spread, reach, pieces=(), kind=jnp.bfloat16):
    values = spread * jax.random.normal(rng, shape, jnp.float32)
    if pieces:
        values = values * block_scale(rng, shape, pieces, -0.22, 0.18)
    return jnp.clip(values, -reach, reach).astype(kind)


def setup_inputs(seed: int = 0, part: int = 0) -> dict:
    seeds = jax.random.split(jax.random.key(seed), 12)
    own_keys = jax.random.split(jax.random.fold_in(seeds[11], part), 12)
    return {
        "tokens": draw_tokens(jax.random.fold_in(jax.random.fold_in(seeds[11], part), 71), part),
        "block_order": jax.random.permutation(seeds[1], NBLOCKS).astype(jnp.int32),
        "doc_lengths": uneven(seeds[2], NDOC, TOKENS, MOST_DOC, 2).astype(jnp.int32),
        "patch_pos": draw_patch_pos(jax.random.fold_in(jax.random.fold_in(seeds[11], part), 71), part),
        "clean_rows": scatter_about(own_keys[4], (PATCHES, D), 1.0, 6.0, ((0, 8),)),
        "w_query": scatter_about(seeds[5], (D, QH * HD), D ** -0.5, 0.078125, ((1, 2),)),
        "q_bias": scatter_about(seeds[6], (QH * HD,), 0.5, 3.0, ((0, 2),)),
        "w_key": scatter_about(seeds[7], (D, KVH * HD), D ** -0.5, 0.078125, ((1, 2),)),
        "k_bias": scatter_about(seeds[8], (KVH * HD,), 0.5, 3.0, ((0, 2),)),
        "w_value": scatter_about(seeds[9], (D, KVH * HD), D ** -0.5, 0.078125, ((1, 2),)),
        "v_bias": scatter_about(seeds[10], (KVH * HD,), 0.5, 3.0, ((0, 2),)),
    }


THETA = 1000000.0


def rotate(head_rows, offset):
    half = head_rows.shape[-1] // 2
    frequency = jnp.power(jnp.float32(THETA), -2.0 * jnp.arange(half, dtype=jnp.float32) / head_rows.shape[-1])
    angles = offset.astype(jnp.float32)[:, None] * frequency[None, :]
    cosines = jnp.cos(angles)[:, None, :]
    sines = jnp.sin(angles)[:, None, :]
    first_half = head_rows[..., :half]
    second_half = head_rows[..., half:]
    return jnp.concatenate([first_half * cosines - second_half * sines, second_half * cosines + first_half * sines], axis=-1)


def project(source, weight, bias, offset, rotated):
    result = jnp.dot(source, weight, preferred_element_type=jnp.float32) + bias.astype(jnp.float32)[None, :]
    if rotated:
        result = rotate(result.reshape(source.shape[0], -1, HD), offset).reshape(source.shape[0], -1)
    return result.astype(jnp.bfloat16)


def slot_places(order, first_row, row_count):
    slots = first_row + jnp.arange(row_count, dtype=jnp.int32)
    owners = slots // BLOCK
    selector = owners[:, None] == jnp.arange(order.shape[0], dtype=jnp.int32)[None, :]
    picked = jnp.sum(jnp.where(selector, order[None, :], 0), axis=1).astype(jnp.int32)
    return picked * BLOCK + slots % BLOCK


def document_info(places, lengths):
    bounds = jnp.cumsum(lengths).astype(jnp.int32)
    passed = places[:, None] >= bounds[None, :]
    documents = jnp.sum(passed.astype(jnp.int32), axis=1).astype(jnp.int32)
    starts = jnp.sum(jnp.where(passed, lengths[None, :], 0), axis=1).astype(jnp.int32)
    return documents, places - starts


def reference(tokens, block_order, doc_lengths, patch_pos, clean_rows, w_query, q_bias, w_key, k_bias, w_value, v_bias):
    places = slot_places(block_order, jnp.int32(0), TOKENS)
    documents, offset = document_info(places, doc_lengths)
    matches = places[:, None] == patch_pos[None, :]
    present = jnp.any(matches, axis=1)
    chosen = jnp.sum(jnp.where(matches, jnp.arange(PATCHES, dtype=jnp.int32)[None, :], 0), axis=1).astype(jnp.int32)
    patched = jnp.where(present[:, None], clean_rows[chosen], tokens)
    group_size = QH // KVH
    query = project(patched, w_query, q_bias, offset, True).reshape(TOKENS, KVH, group_size, HD)
    keys = project(patched, w_key, k_bias, offset, True).reshape(TOKENS, KVH, HD)
    values = project(patched, w_value, v_bias, offset, False).reshape(TOKENS, KVH, HD)
    visible = (documents[:, None] == documents[None, :]) & (places[None, :] <= places[:, None])
    score_scale = HD ** -0.5

    def one_head(operands):
        group_query, head_keys, head_values = operands
        scores = jnp.einsum("tgd,sd->gts", group_query.astype(jnp.float32), head_keys.astype(jnp.float32), precision=lax.Precision.HIGHEST) * score_scale
        masked = jnp.where(visible[None], scores, -1e30)
        peak = jnp.max(masked, axis=-1, keepdims=True)
        weights = jnp.where(visible[None], jnp.exp(masked - peak), 0.0)
        total = jnp.sum(weights, axis=-1)
        rounded = lax.optimization_barrier(weights.astype(jnp.bfloat16))
        mixed = jnp.einsum("gts,sd->tgd", rounded.astype(jnp.float32), head_values.astype(jnp.float32), precision=lax.Precision.HIGHEST)
        return mixed / jnp.transpose(total)[:, :, None]

    outputs = lax.map(one_head, (jnp.transpose(query, (1, 0, 2, 3)), jnp.transpose(keys, (1, 0, 2)), jnp.transpose(values, (1, 0, 2))))
    return jnp.transpose(outputs, (1, 0, 2, 3)).reshape(TOKENS, QH * HD).astype(jnp.bfloat16)
```

```python
import jax
import jax.numpy as jnp
from jax import lax
from jax.sharding import PartitionSpec as P

HD = 128
BLOCK = 64


THETA = 1000000.0


def rotate(head_rows, offset):
    half = head_rows.shape[-1] // 2
    frequency = jnp.power(
        jnp.float32(THETA), -2.0 * jnp.arange(half, dtype=jnp.float32) / head_rows.shape[-1]
    )
    angles = offset.astype(jnp.float32)[:, None] * frequency[None, :]
    cosines = jnp.cos(angles)[:, None, :]
    sines = jnp.sin(angles)[:, None, :]
    first_half = head_rows[..., :half]
    second_half = head_rows[..., half:]
    return jnp.concatenate(
        [first_half * cosines - second_half * sines, second_half * cosines + first_half * sines],
        axis=-1,
    )


def project(source, weight, bias, offset, rotated):
    result = (
        jnp.dot(source, weight, preferred_element_type=jnp.float32)
        + bias.astype(jnp.float32)[None, :]
    )
    if rotated:
        result = rotate(result.reshape(source.shape[0], -1, HD), offset).reshape(
            source.shape[0], -1
        )
    return result.astype(jnp.bfloat16)


def slot_places(order, first_row, row_count):
    slots = first_row + jnp.arange(row_count, dtype=jnp.int32)
    owners = slots // BLOCK
    selector = owners[:, None] == jnp.arange(order.shape[0], dtype=jnp.int32)[None, :]
    picked = jnp.sum(jnp.where(selector, order[None, :], 0), axis=1)
    return picked * BLOCK + slots % BLOCK


def document_info(places, lengths):
    index = jnp.arange(lengths.shape[0], dtype=jnp.int32)
    bounds = jnp.sum(jnp.where(index[:, None] <= index[None, :], lengths[:, None], 0), axis=0)
    passed = places[:, None] >= bounds[None, :]
    documents = jnp.sum(passed.astype(jnp.int32), axis=1)
    starts = jnp.sum(jnp.where(passed, lengths[None, :], 0), axis=1)
    return (documents, places - starts)


def match_patches(places, patch_places):
    matches = places[:, None] == patch_places[None, :]
    present = jnp.any(matches, axis=1)
    chosen = jnp.sum(
        jnp.where(matches, jnp.arange(patch_places.shape[0], dtype=jnp.int32)[None, :], 0), axis=1
    )
    return (present, chosen)


def body(
    tokens,
    block_order,
    doc_lengths,
    patch_pos,
    clean_rows,
    w_query,
    q_bias,
    w_key,
    k_bias,
    w_value,
    v_bias,
):
    local_rows = tokens.shape[0]
    first_row = lax.axis_index("ctx") * local_rows
    places = slot_places(block_order, first_row, local_rows)
    documents, offset = document_info(places, doc_lengths)
    key_heads = w_key.shape[1] // HD
    group_size = w_query.shape[1] // w_key.shape[1]
    gathered_rows, gathered_places = (
        lax.all_gather(clean_rows, "ctx", axis=0, tiled=True),
        lax.all_gather(patch_pos, "ctx", axis=0, tiled=True),
    )
    present, chosen = match_patches(places, gathered_places)
    patched = jnp.where(present[:, None], gathered_rows[chosen], tokens)
    query = project(patched, w_query, q_bias, offset, True)
    keys = project(patched, w_key, k_bias, offset, True)
    values = project(patched, w_value, v_bias, offset, False)
    grouped_query = query.reshape(local_rows, key_heads, group_size, HD)
    score_scale = HD ** (-0.5)

    def attend(running, block_keys, block_values, block_first):
        span_rows = block_keys.shape[0]
        key_places = slot_places(block_order, block_first, span_rows)
        key_documents = document_info(key_places, doc_lengths)[0]
        visible = (documents[:, None] == key_documents[None, :]) & (
            key_places[None, :] <= places[:, None]
        )
        peaks, totals, sums = running
        scores = (
            jnp.einsum(
                "tkgd,skd->tkgs",
                grouped_query,
                block_keys.reshape(span_rows, key_heads, HD),
                preferred_element_type=jnp.float32,
            )
            * score_scale
        )
        shown = visible[:, None, None, :]
        newest = jnp.maximum(peaks, jnp.max(jnp.where(shown, scores, -1e30), axis=-1))
        factor = jnp.exp(peaks - newest)
        weights = jnp.where(shown, jnp.exp(scores - newest[..., None]), 0.0)
        totals = totals * factor + jnp.sum(weights, axis=-1)
        sums = sums * factor[..., None] + jnp.einsum(
            "tkgs,skd->tkgd",
            weights.astype(jnp.bfloat16),
            block_values.reshape(span_rows, key_heads, HD),
            preferred_element_type=jnp.float32,
        )
        return (newest, totals, sums)

    initial = (
        jnp.full((local_rows, key_heads, group_size), -1e30, jnp.float32),
        jnp.zeros((local_rows, key_heads, group_size), jnp.float32),
        jnp.zeros((local_rows, key_heads, group_size, HD), jnp.float32),
    )
    shard_keys = lax.all_gather(keys, "ctx", axis=0, tiled=True)
    shard_values = lax.all_gather(values, "ctx", axis=0, tiled=True)
    total_rows = shard_keys.shape[0]
    span_rows = 512
    blocks_in = total_rows // span_rows

    def advance(previous, current):
        return (attend(previous, current[0], current[1], current[2]), None)

    begins = span_rows * jnp.arange(blocks_in, dtype=jnp.int32)
    stacked_keys = shard_keys.reshape(blocks_in, span_rows, shard_keys.shape[1])
    stacked_values = shard_values.reshape(blocks_in, span_rows, shard_values.shape[1])
    peaks, totals, sums = lax.scan(advance, initial, (stacked_keys, stacked_values, begins))[0]
    return (sums / totals[..., None]).reshape(local_rows, -1).astype(jnp.bfloat16)


def solution(mesh):
    in_specs = (
        P(("run", "ctx"), None),
        P(),
        P(),
        P(("run", "ctx")),
        P(("run", "ctx"), None),
        P(None, "tp"),
        P("tp"),
        P(None, "tp"),
        P("tp"),
        P(None, "tp"),
        P("tp"),
    )
    out_specs = P(("run", "ctx"), "tp")
    return jax.shard_map(body, mesh=mesh, in_specs=in_specs, out_specs=out_specs, check_vma=False)
```

```python
import functools

import jax
import jax.numpy as jnp
from jax import lax
from jax.experimental import pallas as pl
from jax.experimental.pallas import tpu as pltpu
from jax.sharding import PartitionSpec as P

HD = 128
BLOCK = 64
THETA = 1000000.0
CUTS = 2
MESH = pl.DeviceIdType.MESH


def project_kernel(
    n,
    tp,
    pos_ref,
    place_ref,
    cos_ref,
    sin_ref,
    qb_ref,
    kb_ref,
    vb_ref,
    tok_hbm,
    clean_hbm,
    wq_hbm,
    wk_hbm,
    wv_hbm,
    q_out,
    k_out,
    v_out,
    tok,
    clean,
    wq,
    wk,
    wv,
    rows,
    posbuf,
    k_own,
    v_own,
    load_sem,
    zs,
    zr,
    ts,
    tr,
    cs,
    cr,
    ps,
    pr,
    kzs,
    kzr,
    kcs,
    kcr,
    own_sem,
):
    me = lax.axis_index("ctx")
    mine = lax.axis_index("tp")
    nz = n // 2
    z, c = me // 2, lax.rem(me, 2)
    right = lax.rem(z + 1, nz) * 2 + c
    left = lax.rem(z + nz - 1, nz) * 2 + c
    sib = z * 2 + 1 - c
    local, depth = tok.shape
    each = clean_hbm.shape[0]
    half = each // 2
    width = depth // tp
    kvw = wk.shape[1]
    qw = wq.shape[1]
    steps = nz - 1

    loads = [
        pltpu.make_async_copy(clean_hbm, rows.at[pl.ds(pl.multiple_of(me * each, each), each), :], load_sem.at[0]),
        pltpu.make_async_copy(tok_hbm, tok, load_sem.at[1]),
        pltpu.make_async_copy(wk_hbm, wk, load_sem.at[2]),
        pltpu.make_async_copy(wv_hbm, wv, load_sem.at[3]),
        pltpu.make_async_copy(wq_hbm, wq, load_sem.at[4]),
        pltpu.make_async_copy(clean_hbm, clean, load_sem.at[5]),
    ]
    loads[5].start()
    for load in loads[:5]:
        load.start()

    barrier = pltpu.get_barrier_semaphore()
    for k in range(1, n):
        pl.semaphore_signal(barrier, inc=1, device_id={"ctx": lax.rem(me + k, n)}, device_id_type=MESH)
    for k in range(1, tp):
        pl.semaphore_signal(barrier, inc=1, device_id={"tp": lax.rem(mine + k, tp)}, device_id_type=MESH)
    pl.semaphore_wait(barrier, n - 1 + tp - 1)

    def remote(src, dst, send, recv, where):
        return pltpu.make_async_remote_copy(
            src_ref=src, dst_ref=dst, send_sem=send, recv_sem=recv, device_id=where, device_id_type=MESH
        )

    started = []

    def go(copy):
        copy.start()
        started.append(copy)
        return copy

    own_columns = pl.ds(pl.multiple_of(mine * width, 128), width)

    def source(d, s):
        return lax.rem(z - s + nz, nz) * 2 + c if d == 0 else lax.rem(z + s, nz) * 2 + c

    def piece(block, d):
        return pl.ds(pl.multiple_of(block * each + d * half, half), half)

    loads[5].wait()
    for d in range(2):
        go(
            remote(
                clean.at[pl.ds(d * half, half), own_columns],
                rows.at[piece(me, d), own_columns],
                zs.at[d * steps],
                zr.at[d * steps],
                {"ctx": right if d == 0 else left},
            )
        )
    for k in range(1, n):
        go(remote(pos_ref, posbuf.at[me], ps.at[k - 1], pr.at[k - 1], {"ctx": lax.rem(me + k, n)}))
    own_core = go(
        remote(clean, rows.at[pl.ds(pl.multiple_of(me * each, each), each), :], cs.at[2 * steps], cr.at[2 * steps], {"ctx": sib})
    )
    posbuf[me] = pos_ref[...]

    core_copies = []

    def to_core(s):
        for d in range(2):
            region = rows.at[piece(source(d, s + 1), d), :]
            for k in range(1, tp):
                at = (d * steps + s) * (tp - 1) + k - 1
                part = rows.at[
                    piece(source(d, s + 1), d),
                    pl.ds(pl.multiple_of(lax.rem(mine + tp - k, tp) * width, 128), width),
                ]
                remote(part, part, ts.at[at], tr.at[at], {"tp": lax.rem(mine + k, tp)}).wait_recv()
            core_copies.append(go(remote(region, region, cs.at[d * steps + s], cr.at[d * steps + s], {"ctx": sib})))

    for s in range(steps):
        for d in range(2):
            part = rows.at[piece(source(d, s + 1), d), own_columns]
            where = {"ctx": right if d == 0 else left}
            at = d * steps + s
            remote(part, part, zs.at[at], zr.at[at], where).wait_recv()
            if s < steps - 1:
                go(remote(part, part, zs.at[at + 1], zr.at[at + 1], where))
            for k in range(1, tp):
                to = at * (tp - 1) + k - 1
                go(remote(part, part, ts.at[to], tr.at[to], {"tp": lax.rem(mine + k, tp)}))
        if s > 0:
            to_core(s - 1)
    to_core(steps - 1)
    own_core.wait_recv()
    for copy in core_copies:
        copy.wait_recv()
    for k in range(1, n):
        remote(pos_ref, posbuf.at[me], ps.at[k - 1], pr.at[k - 1], {"ctx": me}).wait_recv()
    loads[0].wait()
    loads[1].wait()

    everyone = jnp.max(posbuf[...], axis=0)[0:1, :]
    hits = place_ref[:, 0:1] == everyone
    chosen = jnp.where(hits, 1.0, 0.0).astype(jnp.bfloat16)
    present = jnp.max(jnp.where(hits, 1.0, 0.0), axis=1, keepdims=True) > 0.5
    span = 512

    def patch(j, carry):
        columns = pl.ds(pl.multiple_of(j * span, span), span)
        picked = jnp.dot(chosen, rows[:, columns], preferred_element_type=jnp.float32)
        tok[:, columns] = jnp.where(present, picked, tok[:, columns].astype(jnp.float32)).astype(jnp.bfloat16)
        return carry

    lax.fori_loop(0, depth // span, patch, 0)

    def project(weight, bias, out, rotated):
        total = weight.shape[1]
        tile = 256 if total % 256 == 0 else 128

        def one(j, carry):
            columns = pl.ds(pl.multiple_of(j * tile, tile), tile)
            result = jnp.dot(tok[...], weight[:, columns], preferred_element_type=jnp.float32)
            result = result + bias[:, columns].astype(jnp.float32)
            if rotated:
                parts = []
                for h in range(tile // HD):
                    head = result[:, h * HD : (h + 1) * HD]
                    parts.append(head * cos_ref[...] + pltpu.roll(head, HD // 2, 1) * sin_ref[...])
                result = jnp.concatenate(parts, axis=1) if len(parts) > 1 else parts[0]
            out[:, columns] = result.astype(jnp.bfloat16)
            return carry

        lax.fori_loop(0, total // tile, one, 0)

    cut = local // CUTS

    def slot(block, h):
        return pl.ds(pl.multiple_of(block * local + h * cut, cut), cut)

    def sem_at(d, s, h):
        return (d * nz + s) * CUTS + h

    outs = (k_out, v_out)
    owns = (k_own, v_own)
    own_copies = []

    def send_own(d):
        where = {"ctx": right if d == 0 else left}
        for h in range(CUTS):
            src = owns[d].at[pl.ds(h * cut, cut), :]
            dst = outs[d].at[slot(me, h), :]
            at = sem_at(d, 0, h)
            go(remote(src, dst, kzs.at[at], kzr.at[at], where))
        for h in range(CUTS):
            src = owns[d].at[pl.ds(h * cut, cut), :]
            dst = outs[d].at[slot(me, h), :]
            at = sem_at(d, steps, h)
            go(remote(src, dst, kcs.at[at], kcr.at[at], {"ctx": sib}))
        copy = pltpu.make_async_copy(owns[d], outs[d].at[pl.ds(pl.multiple_of(me * local, local), local), :], own_sem.at[d])
        copy.start()
        own_copies.append(copy)

    loads[2].wait()
    project(wk, kb_ref, k_own, True)
    send_own(0)
    loads[3].wait()
    project(wv, vb_ref, v_own, False)
    send_own(1)
    loads[4].wait()
    project(wq, qb_ref, q_out, True)

    for s in range(steps):
        for h in range(CUTS):
            for d in range(2):
                where = {"ctx": right if d == 0 else left}
                part = outs[d].at[slot(source(d, s + 1), h), :]
                at = sem_at(d, s, h)
                remote(part, part, kzs.at[at], kzr.at[at], where).wait_recv()
                if s < steps - 1:
                    then = sem_at(d, s + 1, h)
                    go(remote(part, part, kzs.at[then], kzr.at[then], where))
                go(remote(part, part, kcs.at[at], kcr.at[at], {"ctx": sib}))
    for s in range(nz):
        for h in range(CUTS):
            for d in range(2):
                at = sem_at(d, s, h)
                part = outs[d].at[slot(source(d, lax.rem(s + 1, nz)) + 1 - 2 * c, h), :]
                remote(part, part, kcs.at[at], kcr.at[at], {"ctx": sib}).wait_recv()
    for copy in own_copies:
        copy.wait()
    for copy in started:
        copy.wait_send()


def attend_kernel(kvh, group, inv_ref, lo_ref, blk_ref, q_ref, k_ref, v_ref, place_ref, start_ref, out_ref, qs, m_s, l_s, acc_s):
    i = pl.program_id(0)
    rows = group * BLOCK
    wide = 4
    keys = wide * BLOCK
    mine = blk_ref[i]
    low = lo_ref[i]
    for h in range(kvh):
        for g in range(group):
            head = h * group + g
            qs[h, g * BLOCK : (g + 1) * BLOCK, :] = q_ref[:, head * HD : (head + 1) * HD]
    m_s[...] = jnp.full_like(m_s, -1e30)
    l_s[...] = jnp.zeros_like(l_s)
    acc_s[...] = jnp.zeros_like(acc_s)
    places = place_ref[:, 0:1]
    starts = start_ref[:, 0:1]

    def step(t, carry):
        first = mine - wide * t - (wide - 1)
        at = [inv_ref[jnp.maximum(first + w, 0)] for w in range(wide)]
        at = [pl.multiple_of(a * BLOCK, BLOCK) for a in at]
        key_places = first * BLOCK + lax.broadcasted_iota(jnp.int32, (BLOCK, keys), 1)
        shown = (key_places >= starts) & (key_places <= places)
        shown = jnp.concatenate([jnp.where(shown, 1.0, 0.0)] * group, axis=0) > 0.5
        for h in range(kvh):
            head = slice(h * HD, (h + 1) * HD)
            k = jnp.concatenate([k_ref[pl.ds(a, BLOCK), head] for a in at], axis=0)
            v = jnp.concatenate([v_ref[pl.ds(a, BLOCK), head] for a in at], axis=0)
            scores = lax.dot_general(
                qs[h], k, (((1,), (1,)), ((), ())), preferred_element_type=jnp.float32
            ) * (HD**-0.5)
            scores = jnp.where(shown, scores, -1e30)
            old = m_s[h][:, 0:1]
            new = jnp.maximum(old, jnp.max(scores, axis=1, keepdims=True))
            factor = jnp.exp(old - new)
            weights = jnp.where(shown, jnp.exp(scores - new), 0.0)
            m_s[h] = jnp.broadcast_to(new, (rows, HD))
            l_s[h] = l_s[h] * factor + jnp.sum(weights, axis=1, keepdims=True)
            acc_s[h] = acc_s[h] * factor + jnp.dot(
                weights.astype(jnp.bfloat16), v, preferred_element_type=jnp.float32
            )
        return carry

    lax.fori_loop(0, (mine - low + wide) // wide, step, 0)
    for h in range(kvh):
        result = (acc_s[h] / l_s[h]).astype(jnp.bfloat16)
        for g in range(group):
            head = h * group + g
            out_ref[:, head * HD : (head + 1) * HD] = result[g * BLOCK : (g + 1) * BLOCK, :]


def body(n, tp, tokens, block_order, doc_lengths, patch_pos, clean_rows, w_query, q_bias, w_key, k_bias, w_value, v_bias):
    local, depth = tokens.shape
    each = patch_pos.shape[0]
    patches = each * n
    qw, kvw = w_query.shape[1], w_key.shape[1]
    kvh = kvw // HD
    group = qw // kvw
    blocks = local // BLOCK
    me = lax.axis_index("ctx")
    nz = n // 2

    ids = jnp.arange(block_order.shape[0], dtype=jnp.int32)
    own_blocks = lax.dynamic_slice(block_order, (me * blocks,), (blocks,))
    inverse = jnp.sum(jnp.where(block_order[None, :] == ids[:, None], ids[None, :], 0), axis=1)
    places = (own_blocks[:, None] * BLOCK + jnp.arange(BLOCK, dtype=jnp.int32)[None, :]).reshape(local)
    index = jnp.arange(doc_lengths.shape[0], dtype=jnp.int32)
    bounds = jnp.sum(jnp.where(index[:, None] <= index[None, :], doc_lengths[:, None], 0), axis=0)
    passed = places[:, None] >= bounds[None, :]
    starts = jnp.sum(jnp.where(passed, doc_lengths[None, :], 0), axis=1)
    offset = places - starts
    lowest = starts.reshape(blocks, BLOCK)[:, 0] // BLOCK
    frequency = jnp.power(jnp.float32(THETA), -2.0 * jnp.arange(HD // 2, dtype=jnp.float32) / HD)
    angles = offset.astype(jnp.float32)[:, None] * frequency[None, :]
    cosines, sines = jnp.cos(angles), jnp.sin(angles)
    cos_all = jnp.concatenate([cosines, cosines], axis=1)
    sin_all = jnp.concatenate([-sines, sines], axis=1)
    place_wide = jnp.broadcast_to(places[:, None], (local, HD))
    start_wide = jnp.broadcast_to(starts[:, None], (local, HD))
    lane = jnp.arange(patches, dtype=jnp.int32)
    pos_row = jnp.where(lane // each == me, jnp.tile(patch_pos, n), -1)
    pos_wide = jnp.broadcast_to(pos_row[None, :], (8, patches))

    vmem = pl.BlockSpec(memory_space=pltpu.VMEM)
    hbm = pl.BlockSpec(memory_space=pl.ANY)
    dma = pltpu.SemaphoreType.DMA
    steps = nz - 1
    query, keys, values = pl.pallas_call(
        functools.partial(project_kernel, n, tp),
        out_shape=(
            jax.ShapeDtypeStruct((local, qw), jnp.bfloat16),
            jax.ShapeDtypeStruct((n * local, kvw), jnp.bfloat16),
            jax.ShapeDtypeStruct((n * local, kvw), jnp.bfloat16),
        ),
        in_specs=[vmem] * 7 + [hbm] * 5,
        out_specs=(vmem, hbm, hbm),
        scratch_shapes=[
            pltpu.VMEM((local, depth), jnp.bfloat16),
            pltpu.VMEM((each, depth), jnp.bfloat16),
            pltpu.VMEM((depth, qw), jnp.bfloat16),
            pltpu.VMEM((depth, kvw), jnp.bfloat16),
            pltpu.VMEM((depth, kvw), jnp.bfloat16),
            pltpu.VMEM((patches, depth), jnp.bfloat16),
            pltpu.VMEM((n, 8, patches), jnp.int32),
            pltpu.VMEM((local, kvw), jnp.bfloat16),
            pltpu.VMEM((local, kvw), jnp.bfloat16),
            dma((6,)),
            dma((2 * steps,)),
            dma((2 * steps,)),
            dma((2 * steps * (tp - 1),)),
            dma((2 * steps * (tp - 1),)),
            dma((2 * steps + 1,)),
            dma((2 * steps + 1,)),
            dma((n - 1,)),
            dma((n - 1,)),
            dma((2 * nz * CUTS,)),
            dma((2 * nz * CUTS,)),
            dma((2 * nz * CUTS,)),
            dma((2 * nz * CUTS,)),
            dma((2,)),
        ],
        compiler_params=pltpu.CompilerParams(
            collective_id=0, has_side_effects=True, vmem_limit_bytes=58 * 1024 * 1024
        ),
        cost_estimate=pl.CostEstimate(
            flops=2 * local * depth * (qw + 2 * kvw), bytes_accessed=2 * depth * (qw + 2 * kvw), transcendentals=0
        ),
    )(
        pos_wide,
        place_wide,
        cos_all,
        sin_all,
        q_bias[None, :],
        k_bias[None, :],
        v_bias[None, :],
        tokens,
        clean_rows,
        w_query,
        w_key,
        w_value,
    )

    whole = lambda i, *_: (0, 0)
    part = lambda i, *_: (i, 0)
    return pl.pallas_call(
        functools.partial(attend_kernel, kvh, group),
        out_shape=jax.ShapeDtypeStruct((local, qw), jnp.bfloat16),
        grid_spec=pltpu.PrefetchScalarGridSpec(
            num_scalar_prefetch=3,
            grid=(blocks,),
            in_specs=[
                pl.BlockSpec((BLOCK, qw), part),
                pl.BlockSpec((n * local, kvw), whole),
                pl.BlockSpec((n * local, kvw), whole),
                pl.BlockSpec((BLOCK, HD), part),
                pl.BlockSpec((BLOCK, HD), part),
            ],
            out_specs=pl.BlockSpec((BLOCK, qw), part),
            scratch_shapes=[
                pltpu.VMEM((kvh, group * BLOCK, HD), jnp.bfloat16),
                pltpu.VMEM((kvh, group * BLOCK, HD), jnp.float32),
                pltpu.VMEM((kvh, group * BLOCK, HD), jnp.float32),
                pltpu.VMEM((kvh, group * BLOCK, HD), jnp.float32),
            ],
        ),
        compiler_params=pltpu.CompilerParams(vmem_limit_bytes=40 * 1024 * 1024),
        cost_estimate=pl.CostEstimate(flops=10**9, bytes_accessed=6 * 10**6, transcendentals=10**6),
    )(inverse, lowest, own_blocks, query, keys, values, place_wide, start_wide)


def solution(mesh):
    in_specs = (
        P(("run", "ctx"), None),
        P(),
        P(),
        P(("run", "ctx")),
        P(("run", "ctx"), None),
        P(None, "tp"),
        P("tp"),
        P(None, "tp"),
        P("tp"),
        P(None, "tp"),
        P("tp"),
    )
    out_specs = P(("run", "ctx"), "tp")
    return jax.shard_map(
        functools.partial(body, mesh.shape["ctx"], mesh.shape["tp"]),
        mesh=mesh,
        in_specs=in_specs,
        out_specs=out_specs,
        check_vma=False,
    )
```

```python
import functools

import jax
import jax.numpy as jnp
import numpy as np
from jax import lax
from jax.experimental import pallas as pl
from jax.experimental.pallas import tpu as pltpu
from jax.sharding import PartitionSpec as P

HD = 128
BLOCK = 64
THETA = 1000000.0
CUTS = 2
MESH = pl.DeviceIdType.MESH


def block_places(block, length_ref):
    place = block * BLOCK + lax.broadcasted_iota(jnp.int32, (BLOCK, HD), 0)
    start = jnp.zeros((BLOCK, HD), jnp.int32)
    bound = jnp.int32(0)
    for j in range(length_ref.shape[0]):
        bound = bound + length_ref[j]
        start = jnp.where(place >= bound, bound, start)
    return place, start


def project_kernel(
    n,
    tp,
    order_ref,
    length_ref,
    patch_ref,
    freq_ref,
    bias_ref,
    tok_hbm,
    clean_hbm,
    wq_hbm,
    wk_hbm,
    wv_hbm,
    q_hbm,
    k_out,
    v_out,
    place_ref,
    cos_ref,
    sin_ref,
    pos_ref,
    q_out,
    tok,
    clean,
    wq,
    wk,
    wv,
    rows,
    posbuf,
    k_own,
    v_own,
    load_sem,
    zs,
    zr,
    ts,
    tr,
    cs,
    cr,
    ps,
    pr,
    kzs,
    kzr,
    kcs,
    kcr,
    own_sem,
):
    me = lax.axis_index("ctx")
    mine = lax.axis_index("tp")
    nz = n // 2
    z, c = me // 2, lax.rem(me, 2)
    right = lax.rem(z + 1, nz) * 2 + c
    left = lax.rem(z + nz - 1, nz) * 2 + c
    sib = z * 2 + 1 - c
    local, depth = tok.shape
    each = clean_hbm.shape[0]
    half = each // 2
    width = depth // tp
    kvw = wk.shape[1]
    qw = wq.shape[1]
    steps = nz - 1

    loads = [
        pltpu.make_async_copy(clean_hbm, rows.at[pl.ds(pl.multiple_of(me * each, each), each), :], load_sem.at[0]),
        pltpu.make_async_copy(tok_hbm, tok, load_sem.at[1]),
        pltpu.make_async_copy(wk_hbm, wk, load_sem.at[2]),
        pltpu.make_async_copy(wv_hbm, wv, load_sem.at[3]),
        pltpu.make_async_copy(wq_hbm, wq, load_sem.at[4]),
        pltpu.make_async_copy(clean_hbm, clean, load_sem.at[5]),
    ]
    loads[5].start()
    for load in loads[:5]:
        load.start()

    barrier = pltpu.get_barrier_semaphore()
    for k in range(1, n):
        pl.semaphore_signal(barrier, inc=1, device_id={"ctx": lax.rem(me + k, n)}, device_id_type=MESH)
    for k in range(1, tp):
        pl.semaphore_signal(barrier, inc=1, device_id={"tp": lax.rem(mine + k, tp)}, device_id_type=MESH)
    pl.semaphore_wait(barrier, n - 1 + tp - 1)

    def remote(src, dst, send, recv, where):
        return pltpu.make_async_remote_copy(
            src_ref=src, dst_ref=dst, send_sem=send, recv_sem=recv, device_id=where, device_id_type=MESH
        )

    started = []

    def go(copy):
        copy.start()
        started.append(copy)
        return copy

    own_columns = pl.ds(pl.multiple_of(mine * width, 128), width)

    def source(d, s):
        return lax.rem(z - s + nz, nz) * 2 + c if d == 0 else lax.rem(z + s, nz) * 2 + c

    def piece(block, d):
        return pl.ds(pl.multiple_of(block * each + d * half, half), half)

    lane = lax.broadcasted_iota(jnp.int32, pos_ref.shape, 1)

    def put(j, row):
        return jnp.where(lane == me * each + j, patch_ref[j], row)

    pos_ref[...] = lax.fori_loop(0, each, put, jnp.full(pos_ref.shape, -1, jnp.int32))
    loads[5].wait()
    for d in range(2):
        go(
            remote(
                clean.at[pl.ds(d * half, half), own_columns],
                rows.at[piece(me, d), own_columns],
                zs.at[d * steps],
                zr.at[d * steps],
                {"ctx": right if d == 0 else left},
            )
        )
    for k in range(1, n):
        go(remote(pos_ref, posbuf.at[me], ps.at[k - 1], pr.at[k - 1], {"ctx": lax.rem(me + k, n)}))
    own_core = go(
        remote(clean, rows.at[pl.ds(pl.multiple_of(me * each, each), each), :], cs.at[2 * steps], cr.at[2 * steps], {"ctx": sib})
    )
    posbuf[me] = pos_ref[...]

    first_half = lax.broadcasted_iota(jnp.int32, (BLOCK, HD), 1) < HD // 2
    for b in range(local // BLOCK):
        place, start = block_places(order_ref[me * (local // BLOCK) + b], length_ref)
        angles = (place - start).astype(jnp.float32) * freq_ref[...]
        here = pl.ds(b * BLOCK, BLOCK)
        place_ref[here, :] = place
        cos_ref[here, :] = jnp.cos(angles)
        sines = jnp.sin(angles)
        sin_ref[here, :] = jnp.where(first_half, -sines, sines)

    core_copies = []

    def to_core(s):
        for d in range(2):
            region = rows.at[piece(source(d, s + 1), d), :]
            for k in range(1, tp):
                at = (d * steps + s) * (tp - 1) + k - 1
                part = rows.at[
                    piece(source(d, s + 1), d),
                    pl.ds(pl.multiple_of(lax.rem(mine + tp - k, tp) * width, 128), width),
                ]
                remote(part, part, ts.at[at], tr.at[at], {"tp": lax.rem(mine + k, tp)}).wait_recv()
            core_copies.append(go(remote(region, region, cs.at[d * steps + s], cr.at[d * steps + s], {"ctx": sib})))

    for s in range(steps):
        for d in range(2):
            part = rows.at[piece(source(d, s + 1), d), own_columns]
            where = {"ctx": right if d == 0 else left}
            at = d * steps + s
            remote(part, part, zs.at[at], zr.at[at], where).wait_recv()
            if s < steps - 1:
                go(remote(part, part, zs.at[at + 1], zr.at[at + 1], where))
            for k in range(1, tp):
                to = at * (tp - 1) + k - 1
                go(remote(part, part, ts.at[to], tr.at[to], {"tp": lax.rem(mine + k, tp)}))
        if s > 0:
            to_core(s - 1)
    to_core(steps - 1)
    own_core.wait_recv()
    for copy in core_copies:
        copy.wait_recv()
    for k in range(1, n):
        remote(pos_ref, posbuf.at[me], ps.at[k - 1], pr.at[k - 1], {"ctx": me}).wait_recv()
    loads[0].wait()
    loads[1].wait()

    everyone = jnp.max(posbuf[...], axis=0)[0:1, :]
    hits = place_ref[:, 0:1] == everyone
    chosen = jnp.where(hits, 1.0, 0.0).astype(jnp.bfloat16)
    present = jnp.max(jnp.where(hits, 1.0, 0.0), axis=1, keepdims=True) > 0.5
    span = 512

    def patch(j, carry):
        columns = pl.ds(pl.multiple_of(j * span, span), span)
        picked = jnp.dot(chosen, rows[:, columns], preferred_element_type=jnp.float32)
        tok[:, columns] = jnp.where(present, picked, tok[:, columns].astype(jnp.float32)).astype(jnp.bfloat16)
        return carry

    lax.fori_loop(0, depth // span, patch, 0)

    def project(weight, base, out, rotated):
        total = weight.shape[1]
        tile = 256 if total % 256 == 0 else 128

        def one(j, carry):
            columns = pl.ds(pl.multiple_of(j * tile, tile), tile)
            result = jnp.dot(tok[...], weight[:, columns], preferred_element_type=jnp.float32)
            result = result + bias_ref[:, pl.ds(pl.multiple_of(base + j * tile, HD), tile)]
            if rotated:
                parts = []
                for h in range(tile // HD):
                    head = result[:, h * HD : (h + 1) * HD]
                    parts.append(head * cos_ref[...] + pltpu.roll(head, HD // 2, 1) * sin_ref[...])
                result = jnp.concatenate(parts, axis=1) if len(parts) > 1 else parts[0]
            out[:, columns] = result.astype(jnp.bfloat16)
            return carry

        lax.fori_loop(0, total // tile, one, 0)

    cut = local // CUTS

    def slot(block, h):
        return pl.ds(pl.multiple_of(block * local + h * cut, cut), cut)

    def sem_at(d, s, h):
        return (d * nz + s) * CUTS + h

    outs = (k_out, v_out)
    owns = (k_own, v_own)
    own_copies = []

    def send_own(d):
        where = {"ctx": right if d == 0 else left}
        for h in range(CUTS):
            src = owns[d].at[pl.ds(h * cut, cut), :]
            dst = outs[d].at[slot(me, h), :]
            at = sem_at(d, 0, h)
            go(remote(src, dst, kzs.at[at], kzr.at[at], where))
        for h in range(CUTS):
            src = owns[d].at[pl.ds(h * cut, cut), :]
            dst = outs[d].at[slot(me, h), :]
            at = sem_at(d, steps, h)
            go(remote(src, dst, kcs.at[at], kcr.at[at], {"ctx": sib}))
        copy = pltpu.make_async_copy(owns[d], outs[d].at[pl.ds(pl.multiple_of(me * local, local), local), :], own_sem.at[d])
        copy.start()
        own_copies.append(copy)

    loads[2].wait()
    project(wk, qw, k_own, True)
    send_own(0)
    loads[3].wait()
    project(wv, qw + kvw, v_own, False)
    send_own(1)
    loads[4].wait()
    project(wq, 0, q_out, True)
    q_copy = pltpu.make_async_copy(q_out, q_hbm, own_sem.at[2])
    q_copy.start()
    own_copies.append(q_copy)

    for s in range(steps):
        for h in range(CUTS):
            for d in range(2):
                where = {"ctx": right if d == 0 else left}
                part = outs[d].at[slot(source(d, s + 1), h), :]
                at = sem_at(d, s, h)
                remote(part, part, kzs.at[at], kzr.at[at], where).wait_recv()
                if s < steps - 1:
                    then = sem_at(d, s + 1, h)
                    go(remote(part, part, kzs.at[then], kzr.at[then], where))
                go(remote(part, part, kcs.at[at], kcr.at[at], {"ctx": sib}))
    for s in range(nz):
        for h in range(CUTS):
            for d in range(2):
                at = sem_at(d, s, h)
                part = outs[d].at[slot(source(d, lax.rem(s + 1, nz)) + 1 - 2 * c, h), :]
                remote(part, part, kcs.at[at], kcr.at[at], {"ctx": sib}).wait_recv()
    for copy in own_copies:
        copy.wait()
    for copy in started:
        copy.wait_send()


def attend_kernel(kvh, group, order_ref, length_ref, q_ref, k_ref, v_ref, out_ref, inv, qs, m_s, l_s, acc_s):
    i = pl.program_id(0)
    wide = 4
    keys = wide * BLOCK
    base = lax.axis_index("ctx") * pl.num_programs(0)

    @pl.when(i == 0)
    def _():
        def put(j, carry):
            inv[order_ref[j]] = j
            return carry

        lax.fori_loop(0, order_ref.shape[0], put, 0)

    mine = order_ref[base + i]
    bound = jnp.int32(0)
    first_start = jnp.int32(0)
    for j in range(length_ref.shape[0]):
        bound = bound + length_ref[j]
        first_start = jnp.where(mine * BLOCK >= bound, bound, first_start)
    low = first_start // BLOCK
    for h in range(kvh):
        for g in range(group):
            head = h * group + g
            qs[h, g * BLOCK : (g + 1) * BLOCK, :] = q_ref[:, head * HD : (head + 1) * HD]
    m_s[...] = jnp.full_like(m_s, -1e30)
    l_s[...] = jnp.zeros_like(l_s)
    acc_s[...] = jnp.zeros_like(acc_s)
    places, starts = block_places(mine, length_ref)
    exponent = HD**-0.5 * 1.4426950408889634

    def step(t, carry):
        first = mine - wide * t - (wide - 1)
        at = [inv[jnp.maximum(first + w, 0)] for w in range(wide)]
        at = [pl.multiple_of(a * BLOCK, BLOCK) for a in at]
        lanes = first * BLOCK + lax.broadcasted_iota(jnp.int32, (BLOCK, HD), 1)
        bias = []
        for w in range(keys // HD):
            shown = (lanes + w * HD >= starts) & (lanes + w * HD <= places)
            bias.append(jnp.where(shown, 0.0, -1e30))
        bias = jnp.concatenate([jnp.concatenate(bias, axis=1)] * group, axis=0)
        for h in range(kvh):
            head = slice(h * HD, (h + 1) * HD)
            k = jnp.concatenate([k_ref[pl.ds(a, BLOCK), head] for a in at], axis=0)
            v = jnp.concatenate([v_ref[pl.ds(a, BLOCK), head] for a in at], axis=0)
            scores = bias + lax.dot_general(
                qs[h], k, (((1,), (1,)), ((), ())), preferred_element_type=jnp.float32
            )
            old = m_s[h]
            new = jnp.maximum(old, jnp.max(scores, axis=1, keepdims=True))
            factor = jnp.exp2((old - new) * exponent)
            weights = jnp.exp2((scores - jnp.concatenate([new] * (keys // HD), axis=1)) * exponent)
            m_s[h] = new
            total = weights[:, :HD]
            for w in range(1, keys // HD):
                total = total + weights[:, w * HD : (w + 1) * HD]
            l_s[h] = l_s[h] * factor + total
            acc_s[h] = acc_s[h] * factor + jnp.dot(
                weights.astype(jnp.bfloat16), v, preferred_element_type=jnp.float32
            )
        return carry

    lax.fori_loop(0, (mine - low + wide) // wide, step, 0)
    for h in range(kvh):
        result = (acc_s[h] / jnp.sum(l_s[h], axis=1, keepdims=True)).astype(jnp.bfloat16)
        for g in range(group):
            head = h * group + g
            out_ref[:, head * HD : (head + 1) * HD] = result[g * BLOCK : (g + 1) * BLOCK, :]


def body(n, tp, tokens, block_order, doc_lengths, patch_pos, clean_rows, w_query, q_bias, w_key, k_bias, w_value, v_bias):
    local, depth = tokens.shape
    each = patch_pos.shape[0]
    patches = each * n
    qw, kvw = w_query.shape[1], w_key.shape[1]
    kvh = kvw // HD
    group = qw // kvw
    blocks = local // BLOCK
    nz = n // 2
    halves = np.float64(THETA) ** (-2.0 * np.arange(HD // 2) / HD)
    frequency = jnp.asarray(np.concatenate([halves, halves])[None, :].astype(np.float32))
    bias = lax.optimization_barrier(
        jnp.concatenate([q_bias.astype(jnp.float32), k_bias.astype(jnp.float32), v_bias.astype(jnp.float32)])
    )[None, :]

    smem = pl.BlockSpec(memory_space=pltpu.SMEM)
    vmem = pl.BlockSpec(memory_space=pltpu.VMEM)
    hbm = pl.BlockSpec(memory_space=pl.ANY)
    dma = pltpu.SemaphoreType.DMA
    steps = nz - 1
    query, keys, values = pl.pallas_call(
        functools.partial(project_kernel, n, tp),
        out_shape=(
            jax.ShapeDtypeStruct((local, qw), jnp.bfloat16),
            jax.ShapeDtypeStruct((n * local, kvw), jnp.bfloat16),
            jax.ShapeDtypeStruct((n * local, kvw), jnp.bfloat16),
        ),
        in_specs=[smem] * 3 + [vmem] * 2 + [hbm] * 5,
        out_specs=(hbm, hbm, hbm),
        scratch_shapes=[
            pltpu.VMEM((local, HD), jnp.int32),
            pltpu.VMEM((local, HD), jnp.float32),
            pltpu.VMEM((local, HD), jnp.float32),
            pltpu.VMEM((8, patches), jnp.int32),
            pltpu.VMEM((local, qw), jnp.bfloat16),
            pltpu.VMEM((local, depth), jnp.bfloat16),
            pltpu.VMEM((each, depth), jnp.bfloat16),
            pltpu.VMEM((depth, qw), jnp.bfloat16),
            pltpu.VMEM((depth, kvw), jnp.bfloat16),
            pltpu.VMEM((depth, kvw), jnp.bfloat16),
            pltpu.VMEM((patches, depth), jnp.bfloat16),
            pltpu.VMEM((n, 8, patches), jnp.int32),
            pltpu.VMEM((local, kvw), jnp.bfloat16),
            pltpu.VMEM((local, kvw), jnp.bfloat16),
            dma((6,)),
            dma((2 * steps,)),
            dma((2 * steps,)),
            dma((2 * steps * (tp - 1),)),
            dma((2 * steps * (tp - 1),)),
            dma((2 * steps + 1,)),
            dma((2 * steps + 1,)),
            dma((n - 1,)),
            dma((n - 1,)),
            dma((2 * nz * CUTS,)),
            dma((2 * nz * CUTS,)),
            dma((2 * nz * CUTS,)),
            dma((2 * nz * CUTS,)),
            dma((3,)),
        ],
        compiler_params=pltpu.CompilerParams(
            collective_id=0, has_side_effects=True, vmem_limit_bytes=58 * 1024 * 1024
        ),
        cost_estimate=pl.CostEstimate(
            flops=2 * local * depth * (qw + 2 * kvw), bytes_accessed=2 * depth * (qw + 2 * kvw), transcendentals=0
        ),
    )(
        block_order,
        doc_lengths,
        patch_pos,
        frequency,
        bias,
        tokens,
        clean_rows,
        w_query,
        w_key,
        w_value,
    )

    whole = lambda i, *_: (0, 0)
    part = lambda i, *_: (i, 0)
    return pl.pallas_call(
        functools.partial(attend_kernel, kvh, group),
        out_shape=jax.ShapeDtypeStruct((local, qw), jnp.bfloat16),
        grid_spec=pltpu.PrefetchScalarGridSpec(
            num_scalar_prefetch=2,
            grid=(blocks,),
            in_specs=[
                pl.BlockSpec((BLOCK, qw), part),
                pl.BlockSpec((n * local, kvw), whole),
                pl.BlockSpec((n * local, kvw), whole),
            ],
            out_specs=pl.BlockSpec((BLOCK, qw), part),
            scratch_shapes=[
                pltpu.SMEM((n * local // BLOCK,), jnp.int32),
                pltpu.VMEM((kvh, group * BLOCK, HD), jnp.bfloat16),
                pltpu.VMEM((kvh, group * BLOCK, HD), jnp.float32),
                pltpu.VMEM((kvh, group * BLOCK, HD), jnp.float32),
                pltpu.VMEM((kvh, group * BLOCK, HD), jnp.float32),
            ],
        ),
        compiler_params=pltpu.CompilerParams(vmem_limit_bytes=60 * 1024 * 1024),
        cost_estimate=pl.CostEstimate(flops=10**9, bytes_accessed=6 * 10**6, transcendentals=10**6),
    )(block_order, doc_lengths, query, keys, values)


def solution(mesh):
    in_specs = (
        P(("run", "ctx"), None),
        P(),
        P(),
        P(("run", "ctx")),
        P(("run", "ctx"), None),
        P(None, "tp"),
        P("tp"),
        P(None, "tp"),
        P("tp"),
        P(None, "tp"),
        P("tp"),
    )
    out_specs = P(("run", "ctx"), "tp")
    return jax.shard_map(
        functools.partial(body, mesh.shape["ctx"], mesh.shape["tp"]),
        mesh=mesh,
        in_specs=in_specs,
        out_specs=out_specs,
        check_vma=False,
    )
```

```python
import functools

import jax
import jax.numpy as jnp
import numpy as np
from jax import lax
from jax.experimental import pallas as pl
from jax.experimental.pallas import tpu as pltpu
from jax.sharding import PartitionSpec as P

HD = 128
BLOCK = 64
THETA = 1000000.0
CUTS = 2
MESH = pl.DeviceIdType.MESH


def block_places(block, length_ref):
    place = block * BLOCK + lax.broadcasted_iota(jnp.int32, (BLOCK, HD), 0)
    start = jnp.zeros((BLOCK, HD), jnp.int32)
    bound = jnp.int32(0)
    for j in range(length_ref.shape[0]):
        bound = bound + length_ref[j]
        start = jnp.where(place >= bound, bound, start)
    return place, start


def project_kernel(
    n,
    tp,
    order_ref,
    length_ref,
    patch_ref,
    freq_ref,
    bias_ref,
    tok_hbm,
    clean_hbm,
    wq_hbm,
    wk_hbm,
    wv_hbm,
    q_hbm,
    k_out,
    v_out,
    place_ref,
    cos_ref,
    sin_ref,
    pos_ref,
    q_out,
    tok,
    clean,
    wq,
    wk,
    wv,
    rows,
    posbuf,
    k_own,
    v_own,
    load_sem,
    zs,
    zr,
    ts,
    tr,
    cs,
    cr,
    ps,
    pr,
    kzs,
    kzr,
    kcs,
    kcr,
    own_sem,
):
    me = lax.axis_index("ctx")
    mine = lax.axis_index("tp")
    nz = n // 2
    z, c = me // 2, lax.rem(me, 2)
    right = lax.rem(z + 1, nz) * 2 + c
    left = lax.rem(z + nz - 1, nz) * 2 + c
    sib = z * 2 + 1 - c
    local, depth = tok.shape
    each = clean_hbm.shape[0]
    half = each // 2
    width = depth // tp
    kvw = wk.shape[1]
    qw = wq.shape[1]
    steps = nz - 1

    loads = [
        pltpu.make_async_copy(clean_hbm, rows.at[pl.ds(pl.multiple_of(me * each, each), each), :], load_sem.at[0]),
        pltpu.make_async_copy(tok_hbm, tok, load_sem.at[1]),
        pltpu.make_async_copy(wk_hbm, wk, load_sem.at[2]),
        pltpu.make_async_copy(wv_hbm, wv, load_sem.at[3]),
        pltpu.make_async_copy(wq_hbm, wq, load_sem.at[4]),
        pltpu.make_async_copy(clean_hbm, clean, load_sem.at[5]),
    ]
    loads[5].start()
    for load in loads[:5]:
        load.start()

    barrier = pltpu.get_barrier_semaphore()
    for k in range(1, n):
        pl.semaphore_signal(barrier, inc=1, device_id={"ctx": lax.rem(me + k, n)}, device_id_type=MESH)
    for k in range(1, tp):
        pl.semaphore_signal(barrier, inc=1, device_id={"tp": lax.rem(mine + k, tp)}, device_id_type=MESH)
    pl.semaphore_wait(barrier, n - 1 + tp - 1)

    def remote(src, dst, send, recv, where):
        return pltpu.make_async_remote_copy(
            src_ref=src, dst_ref=dst, send_sem=send, recv_sem=recv, device_id=where, device_id_type=MESH
        )

    started = []

    def go(copy):
        copy.start()
        started.append(copy)
        return copy

    own_columns = pl.ds(pl.multiple_of(mine * width, 128), width)

    def source(d, s):
        return lax.rem(z - s + nz, nz) * 2 + c if d == 0 else lax.rem(z + s, nz) * 2 + c

    def piece(block, d):
        return pl.ds(pl.multiple_of(block * each + d * half, half), half)

    lane = lax.broadcasted_iota(jnp.int32, pos_ref.shape, 1)

    def put(j, row):
        return jnp.where(lane == me * each + j, patch_ref[j], row)

    pos_ref[...] = lax.fori_loop(0, each, put, jnp.full(pos_ref.shape, -1, jnp.int32))
    loads[5].wait()
    for d in range(2):
        go(
            remote(
                clean.at[pl.ds(d * half, half), own_columns],
                rows.at[piece(me, d), own_columns],
                zs.at[d * steps],
                zr.at[d * steps],
                {"ctx": right if d == 0 else left},
            )
        )
    for k in range(1, n):
        go(remote(pos_ref, posbuf.at[me], ps.at[k - 1], pr.at[k - 1], {"ctx": lax.rem(me + k, n)}))
    own_core = go(
        remote(clean, rows.at[pl.ds(pl.multiple_of(me * each, each), each), :], cs.at[2 * steps], cr.at[2 * steps], {"ctx": sib})
    )
    posbuf[me] = pos_ref[...]

    first_half = lax.broadcasted_iota(jnp.int32, (BLOCK, HD), 1) < HD // 2
    for b in range(local // BLOCK):
        place, start = block_places(order_ref[me * (local // BLOCK) + b], length_ref)
        angles = (place - start).astype(jnp.float32) * freq_ref[...]
        here = pl.ds(b * BLOCK, BLOCK)
        place_ref[here, :] = place
        cos_ref[here, :] = jnp.cos(angles)
        sines = jnp.sin(angles)
        sin_ref[here, :] = jnp.where(first_half, -sines, sines)

    core_copies = []

    def to_core(s):
        for d in range(2):
            region = rows.at[piece(source(d, s + 1), d), :]
            for k in range(1, tp):
                at = (d * steps + s) * (tp - 1) + k - 1
                part = rows.at[
                    piece(source(d, s + 1), d),
                    pl.ds(pl.multiple_of(lax.rem(mine + tp - k, tp) * width, 128), width),
                ]
                remote(part, part, ts.at[at], tr.at[at], {"tp": lax.rem(mine + k, tp)}).wait_recv()
            core_copies.append(go(remote(region, region, cs.at[d * steps + s], cr.at[d * steps + s], {"ctx": sib})))

    for s in range(steps):
        for d in range(2):
            part = rows.at[piece(source(d, s + 1), d), own_columns]
            where = {"ctx": right if d == 0 else left}
            at = d * steps + s
            remote(part, part, zs.at[at], zr.at[at], where).wait_recv()
            if s < steps - 1:
                go(remote(part, part, zs.at[at + 1], zr.at[at + 1], where))
            for k in range(1, tp):
                to = at * (tp - 1) + k - 1
                go(remote(part, part, ts.at[to], tr.at[to], {"tp": lax.rem(mine + k, tp)}))
        if s > 0:
            to_core(s - 1)
    to_core(steps - 1)
    own_core.wait_recv()
    for copy in core_copies:
        copy.wait_recv()
    for k in range(1, n):
        remote(pos_ref, posbuf.at[me], ps.at[k - 1], pr.at[k - 1], {"ctx": me}).wait_recv()
    loads[0].wait()
    loads[1].wait()

    everyone = jnp.max(posbuf[...], axis=0)[0:1, :]
    hits = place_ref[:, 0:1] == everyone
    chosen = jnp.where(hits, 1.0, 0.0).astype(jnp.bfloat16)
    present = jnp.max(jnp.where(hits, 1.0, 0.0), axis=1, keepdims=True) > 0.5
    span = 512

    def patch(j, carry):
        columns = pl.ds(pl.multiple_of(j * span, span), span)
        picked = jnp.dot(chosen, rows[:, columns], preferred_element_type=jnp.float32)
        tok[:, columns] = jnp.where(present, picked, tok[:, columns].astype(jnp.float32)).astype(jnp.bfloat16)
        return carry

    lax.fori_loop(0, depth // span, patch, 0)

    def project(weight, base, out, rotated, share=0, shares=1):
        total = weight.shape[1]
        tile = 256 if total % 256 == 0 else 128

        def one(j, carry):
            columns = pl.ds(pl.multiple_of(j * tile, tile), tile)
            result = jnp.dot(tok[...], weight[:, columns], preferred_element_type=jnp.float32)
            result = result + bias_ref[:, pl.ds(pl.multiple_of(base + j * tile, HD), tile)]
            if rotated:
                parts = []
                for h in range(tile // HD):
                    head = result[:, h * HD : (h + 1) * HD]
                    parts.append(head * cos_ref[...] + pltpu.roll(head, HD // 2, 1) * sin_ref[...])
                result = jnp.concatenate(parts, axis=1) if len(parts) > 1 else parts[0]
            out[:, columns] = result.astype(jnp.bfloat16)
            return carry

        tiles = total // tile
        lax.fori_loop(share * tiles // shares, (share + 1) * tiles // shares, one, 0)

    cut = local // CUTS

    def slot(block, h):
        return pl.ds(pl.multiple_of(block * local + h * cut, cut), cut)

    def sem_at(d, s, h):
        return (d * nz + s) * CUTS + h

    outs = (k_out, v_out)
    owns = (k_own, v_own)
    own_copies = []

    def send_own(d):
        where = {"ctx": right if d == 0 else left}
        for h in range(CUTS):
            src = owns[d].at[pl.ds(h * cut, cut), :]
            dst = outs[d].at[slot(me, h), :]
            at = sem_at(d, 0, h)
            go(remote(src, dst, kzs.at[at], kzr.at[at], where))
        for h in range(CUTS):
            src = owns[d].at[pl.ds(h * cut, cut), :]
            dst = outs[d].at[slot(me, h), :]
            at = sem_at(d, steps, h)
            go(remote(src, dst, kcs.at[at], kcr.at[at], {"ctx": sib}))
        copy = pltpu.make_async_copy(owns[d], outs[d].at[pl.ds(pl.multiple_of(me * local, local), local), :], own_sem.at[d])
        copy.start()
        own_copies.append(copy)

    loads[2].wait()
    project(wk, qw, k_own, True)
    send_own(0)
    loads[3].wait()
    project(wv, qw + kvw, v_own, False)
    send_own(1)
    loads[4].wait()

    def pass_on(s, h):
        for d in range(2):
            where = {"ctx": right if d == 0 else left}
            part = outs[d].at[slot(source(d, s + 1), h), :]
            at = sem_at(d, s, h)
            remote(part, part, kzs.at[at], kzr.at[at], where).wait_recv()
            if s < steps - 1:
                then = sem_at(d, s + 1, h)
                go(remote(part, part, kzs.at[then], kzr.at[then], where))
            go(remote(part, part, kcs.at[at], kcr.at[at], {"ctx": sib}))

    pieces = [(s, h) for s in range(steps) for h in range(CUTS)]
    for share in range(CUTS + 1):
        project(wq, 0, q_out, True, share, CUTS + 1)
        if share < CUTS:
            pass_on(*pieces[share])
    q_copy = pltpu.make_async_copy(q_out, q_hbm, own_sem.at[2])
    q_copy.start()
    own_copies.append(q_copy)
    for step_and_cut in pieces[CUTS:]:
        pass_on(*step_and_cut)
    for s in range(nz):
        for h in range(CUTS):
            for d in range(2):
                at = sem_at(d, s, h)
                part = outs[d].at[slot(source(d, lax.rem(s + 1, nz)) + 1 - 2 * c, h), :]
                remote(part, part, kcs.at[at], kcr.at[at], {"ctx": sib}).wait_recv()
    for copy in own_copies:
        copy.wait()
    for copy in started:
        copy.wait_send()


def attend_kernel(kvh, group, order_ref, length_ref, q_ref, k_ref, v_ref, out_ref, inv, qs, m_s, l_s, acc_s):
    i = pl.program_id(0)
    wide = 4
    keys = wide * BLOCK
    base = lax.axis_index("ctx") * pl.num_programs(0)

    @pl.when(i == 0)
    def _():
        def put(j, carry):
            inv[order_ref[j]] = j
            return carry

        lax.fori_loop(0, order_ref.shape[0], put, 0)

    mine = order_ref[base + i]
    bound = jnp.int32(0)
    first_start = jnp.int32(0)
    for j in range(length_ref.shape[0]):
        bound = bound + length_ref[j]
        first_start = jnp.where(mine * BLOCK >= bound, bound, first_start)
    low = first_start // BLOCK
    for h in range(kvh):
        for g in range(group):
            head = h * group + g
            qs[h, g * BLOCK : (g + 1) * BLOCK, :] = q_ref[:, head * HD : (head + 1) * HD]
    m_s[...] = jnp.full_like(m_s, -1e30)
    l_s[...] = jnp.zeros_like(l_s)
    acc_s[...] = jnp.zeros_like(acc_s)
    places, starts = block_places(mine, length_ref)
    exponent = HD**-0.5 * 1.4426950408889634

    def step(t, carry):
        first = mine - wide * t - (wide - 1)
        at = [inv[jnp.maximum(first + w, 0)] for w in range(wide)]
        at = [pl.multiple_of(a * BLOCK, BLOCK) for a in at]
        lanes = first * BLOCK + lax.broadcasted_iota(jnp.int32, (BLOCK, HD), 1)
        bias = []
        for w in range(keys // HD):
            shown = (lanes + w * HD >= starts) & (lanes + w * HD <= places)
            bias.append(jnp.where(shown, 0.0, -1e30))
        bias = jnp.concatenate([jnp.concatenate(bias, axis=1)] * group, axis=0)
        for h in range(kvh):
            head = slice(h * HD, (h + 1) * HD)
            k = jnp.concatenate([k_ref[pl.ds(a, BLOCK), head] for a in at], axis=0)
            v = jnp.concatenate([v_ref[pl.ds(a, BLOCK), head] for a in at], axis=0)
            scores = bias + lax.dot_general(
                qs[h], k, (((1,), (1,)), ((), ())), preferred_element_type=jnp.float32
            )
            old = m_s[h]
            new = jnp.maximum(old, jnp.max(scores, axis=1, keepdims=True))
            factor = jnp.exp2((old - new) * exponent)
            weights = jnp.exp2((scores - jnp.concatenate([new] * (keys // HD), axis=1)) * exponent)
            m_s[h] = new
            total = weights[:, :HD]
            for w in range(1, keys // HD):
                total = total + weights[:, w * HD : (w + 1) * HD]
            l_s[h] = l_s[h] * factor + total
            acc_s[h] = acc_s[h] * factor + jnp.dot(
                weights.astype(jnp.bfloat16), v, preferred_element_type=jnp.float32
            )
        return carry

    lax.fori_loop(0, (mine - low + wide) // wide, step, 0)
    for h in range(kvh):
        result = (acc_s[h] / jnp.sum(l_s[h], axis=1, keepdims=True)).astype(jnp.bfloat16)
        for g in range(group):
            head = h * group + g
            out_ref[:, head * HD : (head + 1) * HD] = result[g * BLOCK : (g + 1) * BLOCK, :]


def body(n, tp, tokens, block_order, doc_lengths, patch_pos, clean_rows, w_query, q_bias, w_key, k_bias, w_value, v_bias):
    local, depth = tokens.shape
    each = patch_pos.shape[0]
    patches = each * n
    qw, kvw = w_query.shape[1], w_key.shape[1]
    kvh = kvw // HD
    group = qw // kvw
    blocks = local // BLOCK
    nz = n // 2
    halves = np.float64(THETA) ** (-2.0 * np.arange(HD // 2) / HD)
    frequency = jnp.asarray(np.concatenate([halves, halves])[None, :].astype(np.float32))
    bias = lax.optimization_barrier(
        jnp.concatenate([q_bias.astype(jnp.float32), k_bias.astype(jnp.float32), v_bias.astype(jnp.float32)])
    )[None, :]

    smem = pl.BlockSpec(memory_space=pltpu.SMEM)
    vmem = pl.BlockSpec(memory_space=pltpu.VMEM)
    hbm = pl.BlockSpec(memory_space=pl.ANY)
    dma = pltpu.SemaphoreType.DMA
    steps = nz - 1
    query, keys, values = pl.pallas_call(
        functools.partial(project_kernel, n, tp),
        out_shape=(
            jax.ShapeDtypeStruct((local, qw), jnp.bfloat16),
            jax.ShapeDtypeStruct((n * local, kvw), jnp.bfloat16),
            jax.ShapeDtypeStruct((n * local, kvw), jnp.bfloat16),
        ),
        in_specs=[smem] * 3 + [vmem] * 2 + [hbm] * 5,
        out_specs=(hbm, hbm, hbm),
        scratch_shapes=[
            pltpu.VMEM((local, HD), jnp.int32),
            pltpu.VMEM((local, HD), jnp.float32),
            pltpu.VMEM((local, HD), jnp.float32),
            pltpu.VMEM((8, patches), jnp.int32),
            pltpu.VMEM((local, qw), jnp.bfloat16),
            pltpu.VMEM((local, depth), jnp.bfloat16),
            pltpu.VMEM((each, depth), jnp.bfloat16),
            pltpu.VMEM((depth, qw), jnp.bfloat16),
            pltpu.VMEM((depth, kvw), jnp.bfloat16),
            pltpu.VMEM((depth, kvw), jnp.bfloat16),
            pltpu.VMEM((patches, depth), jnp.bfloat16),
            pltpu.VMEM((n, 8, patches), jnp.int32),
            pltpu.VMEM((local, kvw), jnp.bfloat16),
            pltpu.VMEM((local, kvw), jnp.bfloat16),
            dma((6,)),
            dma((2 * steps,)),
            dma((2 * steps,)),
            dma((2 * steps * (tp - 1),)),
            dma((2 * steps * (tp - 1),)),
            dma((2 * steps + 1,)),
            dma((2 * steps + 1,)),
            dma((n - 1,)),
            dma((n - 1,)),
            dma((2 * nz * CUTS,)),
            dma((2 * nz * CUTS,)),
            dma((2 * nz * CUTS,)),
            dma((2 * nz * CUTS,)),
            dma((3,)),
        ],
        compiler_params=pltpu.CompilerParams(
            collective_id=0, has_side_effects=True, vmem_limit_bytes=58 * 1024 * 1024
        ),
        cost_estimate=pl.CostEstimate(
            flops=2 * local * depth * (qw + 2 * kvw), bytes_accessed=2 * depth * (qw + 2 * kvw), transcendentals=0
        ),
    )(
        block_order,
        doc_lengths,
        patch_pos,
        frequency,
        bias,
        tokens,
        clean_rows,
        w_query,
        w_key,
        w_value,
    )

    whole = lambda i, *_: (0, 0)
    part = lambda i, *_: (i, 0)
    return pl.pallas_call(
        functools.partial(attend_kernel, kvh, group),
        out_shape=jax.ShapeDtypeStruct((local, qw), jnp.bfloat16),
        grid_spec=pltpu.PrefetchScalarGridSpec(
            num_scalar_prefetch=2,
            grid=(blocks,),
            in_specs=[
                pl.BlockSpec((BLOCK, qw), part),
                pl.BlockSpec((n * local, kvw), whole),
                pl.BlockSpec((n * local, kvw), whole),
            ],
            out_specs=pl.BlockSpec((BLOCK, qw), part),
            scratch_shapes=[
                pltpu.SMEM((n * local // BLOCK,), jnp.int32),
                pltpu.VMEM((kvh, group * BLOCK, HD), jnp.bfloat16),
                pltpu.VMEM((kvh, group * BLOCK, HD), jnp.float32),
                pltpu.VMEM((kvh, group * BLOCK, HD), jnp.float32),
                pltpu.VMEM((kvh, group * BLOCK, HD), jnp.float32),
            ],
        ),
        compiler_params=pltpu.CompilerParams(vmem_limit_bytes=60 * 1024 * 1024),
        cost_estimate=pl.CostEstimate(flops=10**9, bytes_accessed=6 * 10**6, transcendentals=10**6),
    )(block_order, doc_lengths, query, keys, values)


def solution(mesh):
    in_specs = (
        P(("run", "ctx"), None),
        P(),
        P(),
        P(("run", "ctx")),
        P(("run", "ctx"), None),
        P(None, "tp"),
        P("tp"),
        P(None, "tp"),
        P("tp"),
        P(None, "tp"),
        P("tp"),
    )
    out_specs = P(("run", "ctx"), "tp")
    return jax.shard_map(
        functools.partial(body, mesh.shape["ctx"], mesh.shape["tp"]),
        mesh=mesh,
        in_specs=in_specs,
        out_specs=out_specs,
        check_vma=False,
    )
```

```python
import functools

import jax
import jax.numpy as jnp
import numpy as np
from jax import lax
from jax.experimental import pallas as pl
from jax.experimental.pallas import tpu as pltpu
from jax.sharding import PartitionSpec as P

HD = 128
BLOCK = 64
THETA = 1000000.0
CUTS = 4
MESH = pl.DeviceIdType.MESH


def block_places(block, length_ref):
    place = block * BLOCK + lax.broadcasted_iota(jnp.int32, (BLOCK, HD), 0)
    start = jnp.zeros((BLOCK, HD), jnp.int32)
    bound = jnp.int32(0)
    for j in range(length_ref.shape[0]):
        bound = bound + length_ref[j]
        start = jnp.where(place >= bound, bound, start)
    return place, start


def project_kernel(
    n,
    tp,
    order_ref,
    length_ref,
    patch_ref,
    freq_ref,
    bias_ref,
    tok_hbm,
    clean_hbm,
    wq_hbm,
    wk_hbm,
    wv_hbm,
    q_hbm,
    k_out,
    v_out,
    place_ref,
    cos_ref,
    sin_ref,
    pos_ref,
    q_out,
    tok,
    clean,
    wq,
    wk,
    wv,
    rows,
    posbuf,
    k_own,
    v_own,
    load_sem,
    zs,
    zr,
    ts,
    tr,
    cs,
    cr,
    ps,
    pr,
    kzs,
    kzr,
    kcs,
    kcr,
    own_sem,
):
    me = lax.axis_index("ctx")
    mine = lax.axis_index("tp")
    nz = n // 2
    z, c = me // 2, lax.rem(me, 2)
    right = lax.rem(z + 1, nz) * 2 + c
    left = lax.rem(z + nz - 1, nz) * 2 + c
    sib = z * 2 + 1 - c
    local, depth = tok.shape
    each = clean_hbm.shape[0]
    half = each // 2
    width = depth // tp
    kvw = wk.shape[1]
    qw = wq.shape[1]
    steps = nz - 1

    loads = [
        pltpu.make_async_copy(clean_hbm, rows.at[pl.ds(pl.multiple_of(me * each, each), each), :], load_sem.at[0]),
        pltpu.make_async_copy(tok_hbm, tok, load_sem.at[1]),
        pltpu.make_async_copy(wk_hbm, wk, load_sem.at[2]),
        pltpu.make_async_copy(wv_hbm, wv, load_sem.at[3]),
        pltpu.make_async_copy(wq_hbm, wq, load_sem.at[4]),
        pltpu.make_async_copy(clean_hbm, clean, load_sem.at[5]),
    ]
    loads[5].start()
    for load in loads[:5]:
        load.start()

    barrier = pltpu.get_barrier_semaphore()
    for k in range(1, n):
        pl.semaphore_signal(barrier, inc=1, device_id={"ctx": lax.rem(me + k, n)}, device_id_type=MESH)
    for k in range(1, tp):
        pl.semaphore_signal(barrier, inc=1, device_id={"tp": lax.rem(mine + k, tp)}, device_id_type=MESH)
    pl.semaphore_wait(barrier, n - 1 + tp - 1)

    def remote(src, dst, send, recv, where):
        return pltpu.make_async_remote_copy(
            src_ref=src, dst_ref=dst, send_sem=send, recv_sem=recv, device_id=where, device_id_type=MESH
        )

    started = []

    def go(copy):
        copy.start()
        started.append(copy)
        return copy

    own_columns = pl.ds(pl.multiple_of(mine * width, 128), width)

    def source(d, s):
        return lax.rem(z - s + nz, nz) * 2 + c if d == 0 else lax.rem(z + s, nz) * 2 + c

    def piece(block, d):
        return pl.ds(pl.multiple_of(block * each + d * half, half), half)

    lane = lax.broadcasted_iota(jnp.int32, pos_ref.shape, 1)

    def put(j, row):
        return jnp.where(lane == me * each + j, patch_ref[j], row)

    pos_ref[...] = lax.fori_loop(0, each, put, jnp.full(pos_ref.shape, -1, jnp.int32))
    loads[5].wait()
    for d in range(2):
        go(
            remote(
                clean.at[pl.ds(d * half, half), own_columns],
                rows.at[piece(me, d), own_columns],
                zs.at[d * steps],
                zr.at[d * steps],
                {"ctx": right if d == 0 else left},
            )
        )
    for k in range(1, n):
        go(remote(pos_ref, posbuf.at[me], ps.at[k - 1], pr.at[k - 1], {"ctx": lax.rem(me + k, n)}))
    own_core = go(
        remote(clean, rows.at[pl.ds(pl.multiple_of(me * each, each), each), :], cs.at[2 * steps], cr.at[2 * steps], {"ctx": sib})
    )
    posbuf[me] = pos_ref[...]

    first_half = lax.broadcasted_iota(jnp.int32, (BLOCK, HD), 1) < HD // 2
    for b in range(local // BLOCK):
        place, start = block_places(order_ref[me * (local // BLOCK) + b], length_ref)
        angles = (place - start).astype(jnp.float32) * freq_ref[...]
        here = pl.ds(b * BLOCK, BLOCK)
        place_ref[here, :] = place
        cos_ref[here, :] = jnp.cos(angles)
        sines = jnp.sin(angles)
        sin_ref[here, :] = jnp.where(first_half, -sines, sines)

    core_copies = []

    def to_core(s):
        for d in range(2):
            region = rows.at[piece(source(d, s + 1), d), :]
            for k in range(1, tp):
                at = (d * steps + s) * (tp - 1) + k - 1
                part = rows.at[
                    piece(source(d, s + 1), d),
                    pl.ds(pl.multiple_of(lax.rem(mine + tp - k, tp) * width, 128), width),
                ]
                remote(part, part, ts.at[at], tr.at[at], {"tp": lax.rem(mine + k, tp)}).wait_recv()
            core_copies.append(go(remote(region, region, cs.at[d * steps + s], cr.at[d * steps + s], {"ctx": sib})))

    for s in range(steps):
        for d in range(2):
            part = rows.at[piece(source(d, s + 1), d), own_columns]
            where = {"ctx": right if d == 0 else left}
            at = d * steps + s
            remote(part, part, zs.at[at], zr.at[at], where).wait_recv()
            if s < steps - 1:
                go(remote(part, part, zs.at[at + 1], zr.at[at + 1], where))
            for k in range(1, tp):
                to = at * (tp - 1) + k - 1
                go(remote(part, part, ts.at[to], tr.at[to], {"tp": lax.rem(mine + k, tp)}))
        if s > 0:
            to_core(s - 1)
    to_core(steps - 1)
    own_core.wait_recv()
    for copy in core_copies:
        copy.wait_recv()
    for k in range(1, n):
        remote(pos_ref, posbuf.at[me], ps.at[k - 1], pr.at[k - 1], {"ctx": me}).wait_recv()
    loads[0].wait()
    loads[1].wait()

    everyone = jnp.max(posbuf[...], axis=0)[0:1, :]
    hits = place_ref[:, 0:1] == everyone
    chosen = jnp.where(hits, 1.0, 0.0).astype(jnp.bfloat16)
    present = jnp.max(jnp.where(hits, 1.0, 0.0), axis=1, keepdims=True) > 0.5
    span = 512

    def patch(j, carry):
        columns = pl.ds(pl.multiple_of(j * span, span), span)
        picked = jnp.dot(chosen, rows[:, columns], preferred_element_type=jnp.float32)
        tok[:, columns] = jnp.where(present, picked, tok[:, columns].astype(jnp.float32)).astype(jnp.bfloat16)
        return carry

    lax.fori_loop(0, depth // span, patch, 0)

    def project(weight, base, out, rotated, share=0, shares=1):
        total = weight.shape[1]
        tile = 256 if total % 256 == 0 else 128

        def one(j, carry):
            columns = pl.ds(pl.multiple_of(j * tile, tile), tile)
            result = jnp.dot(tok[...], weight[:, columns], preferred_element_type=jnp.float32)
            result = result + bias_ref[:, pl.ds(pl.multiple_of(base + j * tile, HD), tile)]
            if rotated:
                parts = []
                for h in range(tile // HD):
                    head = result[:, h * HD : (h + 1) * HD]
                    parts.append(head * cos_ref[...] + pltpu.roll(head, HD // 2, 1) * sin_ref[...])
                result = jnp.concatenate(parts, axis=1) if len(parts) > 1 else parts[0]
            out[:, columns] = result.astype(jnp.bfloat16)
            return carry

        tiles = total // tile
        lax.fori_loop(share * tiles // shares, (share + 1) * tiles // shares, one, 0)

    cut = local // CUTS

    def slot(block, h):
        return pl.ds(pl.multiple_of(block * local + h * cut, cut), cut)

    def sem_at(d, s, h):
        return (d * nz + s) * CUTS + h

    outs = (k_out, v_out)
    owns = (k_own, v_own)
    own_copies = []

    def send_own(d):
        where = {"ctx": right if d == 0 else left}
        for h in range(CUTS):
            src = owns[d].at[pl.ds(h * cut, cut), :]
            dst = outs[d].at[slot(me, h), :]
            at = sem_at(d, 0, h)
            go(remote(src, dst, kzs.at[at], kzr.at[at], where))
        for h in range(CUTS):
            src = owns[d].at[pl.ds(h * cut, cut), :]
            dst = outs[d].at[slot(me, h), :]
            at = sem_at(d, steps, h)
            go(remote(src, dst, kcs.at[at], kcr.at[at], {"ctx": sib}))
        copy = pltpu.make_async_copy(owns[d], outs[d].at[pl.ds(pl.multiple_of(me * local, local), local), :], own_sem.at[d])
        copy.start()
        own_copies.append(copy)

    loads[2].wait()
    project(wk, qw, k_own, True)
    send_own(0)
    loads[3].wait()
    project(wv, qw + kvw, v_own, False)
    send_own(1)
    loads[4].wait()

    def pass_on(s, h):
        for d in range(2):
            where = {"ctx": right if d == 0 else left}
            part = outs[d].at[slot(source(d, s + 1), h), :]
            at = sem_at(d, s, h)
            remote(part, part, kzs.at[at], kzr.at[at], where).wait_recv()
            if s < steps - 1:
                then = sem_at(d, s + 1, h)
                go(remote(part, part, kzs.at[then], kzr.at[then], where))
            go(remote(part, part, kcs.at[at], kcr.at[at], {"ctx": sib}))

    pieces = [(s, h) for s in range(steps) for h in range(CUTS)]
    for share in range(CUTS + 1):
        project(wq, 0, q_out, True, share, CUTS + 1)
        if share < CUTS:
            pass_on(*pieces[share])
    q_copy = pltpu.make_async_copy(q_out, q_hbm, own_sem.at[2])
    q_copy.start()
    own_copies.append(q_copy)
    for step_and_cut in pieces[CUTS:]:
        pass_on(*step_and_cut)
    for s in range(nz):
        for h in range(CUTS):
            for d in range(2):
                at = sem_at(d, s, h)
                part = outs[d].at[slot(source(d, lax.rem(s + 1, nz)) + 1 - 2 * c, h), :]
                remote(part, part, kcs.at[at], kcr.at[at], {"ctx": sib}).wait_recv()
    for copy in own_copies:
        copy.wait()
    for copy in started:
        copy.wait_send()


def attend_kernel(kvh, group, order_ref, length_ref, q_ref, k_ref, v_ref, out_ref, inv, qs, m_s, l_s, acc_s):
    i = pl.program_id(0)
    wide = 4
    keys = wide * BLOCK
    base = lax.axis_index("ctx") * pl.num_programs(0)

    @pl.when(i == 0)
    def _():
        def put(j, carry):
            inv[order_ref[j]] = j
            return carry

        lax.fori_loop(0, order_ref.shape[0], put, 0)

    mine = order_ref[base + i]
    bound = jnp.int32(0)
    first_start = jnp.int32(0)
    for j in range(length_ref.shape[0]):
        bound = bound + length_ref[j]
        first_start = jnp.where(mine * BLOCK >= bound, bound, first_start)
    low = first_start // BLOCK
    for h in range(kvh):
        for g in range(group):
            head = h * group + g
            qs[h, g * BLOCK : (g + 1) * BLOCK, :] = q_ref[:, head * HD : (head + 1) * HD]
    m_s[...] = jnp.full_like(m_s, -1e30)
    l_s[...] = jnp.zeros_like(l_s)
    acc_s[...] = jnp.zeros_like(acc_s)
    places, starts = block_places(mine, length_ref)
    exponent = HD**-0.5 * 1.4426950408889634

    def step(t, carry):
        first = mine - wide * t - (wide - 1)
        at = [inv[jnp.maximum(first + w, 0)] for w in range(wide)]
        at = [pl.multiple_of(a * BLOCK, BLOCK) for a in at]
        lanes = first * BLOCK + lax.broadcasted_iota(jnp.int32, (BLOCK, HD), 1)
        bias = []
        for w in range(keys // HD):
            shown = (lanes + w * HD >= starts) & (lanes + w * HD <= places)
            bias.append(jnp.where(shown, 0.0, -1e30))
        bias = jnp.concatenate([jnp.concatenate(bias, axis=1)] * group, axis=0)
        for h in range(kvh):
            head = slice(h * HD, (h + 1) * HD)
            k = jnp.concatenate([k_ref[pl.ds(a, BLOCK), head] for a in at], axis=0)
            v = jnp.concatenate([v_ref[pl.ds(a, BLOCK), head] for a in at], axis=0)
            scores = bias + lax.dot_general(
                qs[h], k, (((1,), (1,)), ((), ())), preferred_element_type=jnp.float32
            )
            old = m_s[h]
            new = jnp.maximum(old, jnp.max(scores, axis=1, keepdims=True))
            factor = jnp.exp2((old - new) * exponent)
            weights = jnp.exp2((scores - jnp.concatenate([new] * (keys // HD), axis=1)) * exponent)
            m_s[h] = new
            total = weights[:, :HD]
            for w in range(1, keys // HD):
                total = total + weights[:, w * HD : (w + 1) * HD]
            l_s[h] = l_s[h] * factor + total
            acc_s[h] = acc_s[h] * factor + jnp.dot(
                weights.astype(jnp.bfloat16), v, preferred_element_type=jnp.float32
            )
        return carry

    lax.fori_loop(0, (mine - low + wide) // wide, step, 0)
    for h in range(kvh):
        result = (acc_s[h] / jnp.sum(l_s[h], axis=1, keepdims=True)).astype(jnp.bfloat16)
        for g in range(group):
            head = h * group + g
            out_ref[:, head * HD : (head + 1) * HD] = result[g * BLOCK : (g + 1) * BLOCK, :]


def body(n, tp, tokens, block_order, doc_lengths, patch_pos, clean_rows, w_query, q_bias, w_key, k_bias, w_value, v_bias):
    local, depth = tokens.shape
    each = patch_pos.shape[0]
    patches = each * n
    qw, kvw = w_query.shape[1], w_key.shape[1]
    kvh = kvw // HD
    group = qw // kvw
    blocks = local // BLOCK
    nz = n // 2
    halves = np.float64(THETA) ** (-2.0 * np.arange(HD // 2) / HD)
    frequency = jnp.asarray(np.concatenate([halves, halves])[None, :].astype(np.float32))
    bias = lax.optimization_barrier(
        jnp.concatenate([q_bias.astype(jnp.float32), k_bias.astype(jnp.float32), v_bias.astype(jnp.float32)])
    )[None, :]

    smem = pl.BlockSpec(memory_space=pltpu.SMEM)
    vmem = pl.BlockSpec(memory_space=pltpu.VMEM)
    hbm = pl.BlockSpec(memory_space=pl.ANY)
    dma = pltpu.SemaphoreType.DMA
    steps = nz - 1
    query, keys, values = pl.pallas_call(
        functools.partial(project_kernel, n, tp),
        out_shape=(
            jax.ShapeDtypeStruct((local, qw), jnp.bfloat16),
            jax.ShapeDtypeStruct((n * local, kvw), jnp.bfloat16),
            jax.ShapeDtypeStruct((n * local, kvw), jnp.bfloat16),
        ),
        in_specs=[smem] * 3 + [vmem] * 2 + [hbm] * 5,
        out_specs=(hbm, hbm, hbm),
        scratch_shapes=[
            pltpu.VMEM((local, HD), jnp.int32),
            pltpu.VMEM((local, HD), jnp.float32),
            pltpu.VMEM((local, HD), jnp.float32),
            pltpu.VMEM((8, patches), jnp.int32),
            pltpu.VMEM((local, qw), jnp.bfloat16),
            pltpu.VMEM((local, depth), jnp.bfloat16),
            pltpu.VMEM((each, depth), jnp.bfloat16),
            pltpu.VMEM((depth, qw), jnp.bfloat16),
            pltpu.VMEM((depth, kvw), jnp.bfloat16),
            pltpu.VMEM((depth, kvw), jnp.bfloat16),
            pltpu.VMEM((patches, depth), jnp.bfloat16),
            pltpu.VMEM((n, 8, patches), jnp.int32),
            pltpu.VMEM((local, kvw), jnp.bfloat16),
            pltpu.VMEM((local, kvw), jnp.bfloat16),
            dma((6,)),
            dma((2 * steps,)),
            dma((2 * steps,)),
            dma((2 * steps * (tp - 1),)),
            dma((2 * steps * (tp - 1),)),
            dma((2 * steps + 1,)),
            dma((2 * steps + 1,)),
            dma((n - 1,)),
            dma((n - 1,)),
            dma((2 * nz * CUTS,)),
            dma((2 * nz * CUTS,)),
            dma((2 * nz * CUTS,)),
            dma((2 * nz * CUTS,)),
            dma((3,)),
        ],
        compiler_params=pltpu.CompilerParams(
            collective_id=0, has_side_effects=True, vmem_limit_bytes=58 * 1024 * 1024
        ),
        cost_estimate=pl.CostEstimate(
            flops=2 * local * depth * (qw + 2 * kvw), bytes_accessed=2 * depth * (qw + 2 * kvw), transcendentals=0
        ),
    )(
        block_order,
        doc_lengths,
        patch_pos,
        frequency,
        bias,
        tokens,
        clean_rows,
        w_query,
        w_key,
        w_value,
    )

    whole = lambda i, *_: (0, 0)
    part = lambda i, *_: (i, 0)
    return pl.pallas_call(
        functools.partial(attend_kernel, kvh, group),
        out_shape=jax.ShapeDtypeStruct((local, qw), jnp.bfloat16),
        grid_spec=pltpu.PrefetchScalarGridSpec(
            num_scalar_prefetch=2,
            grid=(blocks,),
            in_specs=[
                pl.BlockSpec((BLOCK, qw), part),
                pl.BlockSpec((n * local, kvw), whole),
                pl.BlockSpec((n * local, kvw), whole),
            ],
            out_specs=pl.BlockSpec((BLOCK, qw), part),
            scratch_shapes=[
                pltpu.SMEM((n * local // BLOCK,), jnp.int32),
                pltpu.VMEM((kvh, group * BLOCK, HD), jnp.bfloat16),
                pltpu.VMEM((kvh, group * BLOCK, HD), jnp.float32),
                pltpu.VMEM((kvh, group * BLOCK, HD), jnp.float32),
                pltpu.VMEM((kvh, group * BLOCK, HD), jnp.float32),
            ],
        ),
        compiler_params=pltpu.CompilerParams(vmem_limit_bytes=60 * 1024 * 1024),
        cost_estimate=pl.CostEstimate(flops=10**9, bytes_accessed=6 * 10**6, transcendentals=10**6),
    )(block_order, doc_lengths, query, keys, values)


def solution(mesh):
    in_specs = (
        P(("run", "ctx"), None),
        P(),
        P(),
        P(("run", "ctx")),
        P(("run", "ctx"), None),
        P(None, "tp"),
        P("tp"),
        P(None, "tp"),
        P("tp"),
        P(None, "tp"),
        P("tp"),
    )
    out_specs = P(("run", "ctx"), "tp")
    return jax.shard_map(
        functools.partial(body, mesh.shape["ctx"], mesh.shape["tp"]),
        mesh=mesh,
        in_specs=in_specs,
        out_specs=out_specs,
        check_vma=False,
    )
```
